256 devices in a mesh: head: 8 (over y_hi, x), blk: 32 (over y_lo, z, core).
Axes of the slice: x: 4, y: 4 (y_hi: 2, y_lo: 2; y = y_hi * 2 + y_lo), z: 8, core: 2. Of those that a mesh axis runs over, the one named last changes fastest.
Arguments:
- queries: bfloat16 [32768, 3072], P(('blk', 'head')), may hold values from -120 to 120
- keys: bfloat16 [32768, 3072], P(('blk', 'head')), may hold values from -4 to 4
- values: bfloat16 [32768, 3072], P(('blk', 'head')), may hold values from -24 to 24
- text_codes: int32 [2, 256, 3072], P(None, None, 'head'), may hold values from -448 to 448
- text_exps: int32 [2, 256, 24], P(None, None, 'head'), may hold values from -9 to -7
Outputs:
- attended: bfloat16 [32768, 3072], P(('blk', 'head'))
The draws below stay inside these ranges and needn't reach their ends.
All inputs are finite; a program needn't handle non-finite values.
Results may differ from the reference program's by a relative error of at most 0.0077.
Values may be sent and summed in bfloat16 or wider, within the bound.
A program may use at most 128 MiB of HBM per device.

```python
import math
import jax
import jax.numpy as jnp
from jax import lax

H = 24
HD = 128
TEXT = 256
PREV = 3
TOK_DEV = 128
D = 3072
TOKENS = 32768
N_HEAD = 8
N_BLK = 32


def draw_queries(key, part):
    key = jax.random.fold_in(key, 11)
    return jnp.clip(2.0 * jax.random.normal(key, (TOKENS, D), jnp.float32), -8.0, 8.0).astype(jnp.bfloat16)


def draw_keys(key, part):
    key = jax.random.fold_in(key, 12)
    return jnp.clip(jax.random.normal(key, (TOKENS, D), jnp.float32), -4.0, 4.0).astype(jnp.bfloat16)


def touch_ends(array, own_key, least, largest):
    place = [jax.random.randint(jax.random.fold_in(own_key, axis), (), 0, length) for axis, length in enumerate(array.shape)]
    widest = array.shape.index(max(array.shape))
    neighbour = place[:widest] + [(place[widest] + 1) % array.shape[widest]] + place[widest + 1:]
    return array.at[tuple(place)].set(least).at[tuple(neighbour)].set(largest)


def steps_of(rng, dims, split, smallest, top_value):
    loudness, own = 1.0, jax.random.fold_in(rng, 6)
    for dim, shards_of in split:
        draws = jnp.exp(jax.random.uniform(jax.random.fold_in(own, dim), (shards_of,), jnp.float32, smallest / len(split), top_value / len(split)))
        loudness = loudness * jnp.repeat(draws, dims[dim] // shards_of).reshape([-1 if axis == dim else 1 for axis in range(len(dims))])
    return loudness


def bell_draw(stream_key, dims, spread, most, cuts=(), kind=jnp.bfloat16):
    loudness = steps_of(stream_key, dims, cuts, -0.22, 0.18) if cuts else 1.0
    array = jax.random.normal(stream_key, dims, jnp.float32) * spread * loudness
    return jnp.minimum(jnp.maximum(array, -most), most).astype(kind)


def setup_inputs(seed: int = 0) -> dict:
    key_of = jax.random.split(jax.random.key(seed), 6)
    queries = draw_queries(jax.random.fold_in(key_of[5], 71), 0)
    keys = draw_keys(jax.random.fold_in(key_of[5], 71), 0)
    values = bell_draw(key_of[2], (TOKENS, D), 4.0, 24.0, ((0, 256),))
    text_codes = touch_ends(jax.random.randint(key_of[3], (2, TEXT, D), -448, 449), jax.random.fold_in(key_of[3], 1), -448, 448).astype(jnp.int32)
    text_exps = touch_ends(jax.random.randint(key_of[4], (2, TEXT, H), -9, -6), jax.random.fold_in(key_of[4], 1), -9, (-6) - 1).astype(jnp.int32)
    return dict(queries=queries, keys=keys, values=values, text_codes=text_codes, text_exps=text_exps)


def dequantize(codes, exps):
    widened = jnp.repeat(exps.astype(jnp.float32), HD, axis=1)
    return (codes.astype(jnp.float32) * jnp.exp2(widened)).astype(jnp.bfloat16)

def reference(queries, keys, values, text_codes, text_exps):
    softmax_scale = 1.0 / math.sqrt(HD)
    text_keys = dequantize(text_codes[0], text_exps[0])
    text_values = dequantize(text_codes[1], text_exps[1])
    block_rows = TOK_DEV * N_HEAD
    query_blocks = queries.reshape(N_BLK, block_rows, D)
    key_blocks = keys.reshape(N_BLK, block_rows, D)
    value_blocks = values.reshape(N_BLK, block_rows, D)

    def one_block(index):
        picks = ((index - jnp.arange(PREV + 1)) % N_BLK).astype(jnp.int32)
        window_keys = jnp.concatenate([key_blocks[picks].reshape(-1, D), text_keys], axis=0)
        window_values = jnp.concatenate([value_blocks[picks].reshape(-1, D), text_values], axis=0)
        query_rows = query_blocks[index]

        def one_head(head_index):
            start = (head_index * HD).astype(jnp.int32)
            query_head = lax.dynamic_slice_in_dim(query_rows, start, HD, 1)
            key_head = lax.dynamic_slice_in_dim(window_keys, start, HD, 1)
            value_head = lax.dynamic_slice_in_dim(window_values, start, HD, 1)
            scores = jnp.dot(query_head, key_head.T, preferred_element_type=jnp.float32) * softmax_scale
            row_max = lax.optimization_barrier(jnp.max(scores, axis=-1, keepdims=True))
            expo = jnp.exp(scores - row_max)
            total = lax.optimization_barrier(jnp.sum(expo, axis=-1, keepdims=True))
            weights = expo.astype(jnp.bfloat16)
            summed = jnp.dot(weights, value_head, preferred_element_type=jnp.float32)
            return (summed / total).astype(jnp.bfloat16)
        per_head = lax.map(one_head, jnp.arange(H))
        return jnp.transpose(per_head, (1, 0, 2)).reshape(block_rows, D)
    result = lax.map(one_block, jnp.arange(N_BLK))
    return result.reshape(TOKENS, D)
```

```python
import math

import jax
import jax.numpy as jnp
from jax import lax
from jax.experimental import pallas as pl
from jax.experimental.pallas import tpu as pltpu
from jax.sharding import PartitionSpec as P

HD = 128
ROWS = 128
BLOCK = 1024
TEXT = 256
GROUP = 8
N_BLK = 32
PAIRS = 16
A_SLOTS, B_SLOTS = 5, 4
TILE = 256
CHUNK = 512
MESH = pl.DeviceIdType.MESH
SCALE = math.log2(math.e) / math.sqrt(HD)
BF16, F32 = jnp.bfloat16, jnp.float32


def owner(t, p):
    return (t * 8 + p % 8) * 2 + p // 8


def kernel(
    q_in, k_in, v_in, codes_in, exps_in, out,
    qs, ks, vs, tks, tvs, codes, exps, m_s, acc_s, o_s,
    text_sem, k_sem, v_sem, q_sem, out_sem,
    piece_send, own_send, fwd_send, o_send, o_own_send,
):
    me = lax.axis_index("head")
    b = lax.axis_index("blk")
    yl, z, c = b // 16, (b // 2) % 8, b % 2
    pair, pair_q = b // 2, ((b + N_BLK - 1) % N_BLK) // 2
    mine = c * 8 + z
    after, after2 = (b + 1) % N_BLK, (b + 2) % N_BLK
    before, before2 = (b + N_BLK - 1) % N_BLK, (b + N_BLK - 2) % N_BLK
    next_a, prev_a = owner(yl, (mine + 1) % PAIRS), owner(yl, (mine + PAIRS - 1) % PAIRS)

    text_copies = [
        pltpu.make_async_copy(codes_in.at[:, :, pl.ds(pl.multiple_of(yl * HD, HD), HD)], codes.at[0], text_sem.at[0]),
        pltpu.make_async_copy(codes_in.at[:, :, pl.ds(2 * HD, HD)], codes.at[1], text_sem.at[1]),
        pltpu.make_async_copy(exps_in, exps, text_sem.at[2]),
    ]
    for copy in text_copies:
        copy.start()

    barrier = pltpu.get_barrier_semaphore()

    def tell(head, blk):
        pl.semaphore_signal(barrier, inc=1, device_id=(head, blk), device_id_type=MESH)

    def greet(i, _):
        other = (me + 1 + i) % GROUP
        for d in range(3):
            tell(other, (mine * 2 + d) % N_BLK)
        tell(other, b)
        tell(other, after)
        tell(other, before)
        for t in range(2):
            tell(other, owner(t, pair_q))
        return 0

    lax.fori_loop(0, GROUP - 1, greet, 0)
    for d in range(3):

        @pl.when((mine * 2 + d) % N_BLK != b)
        def _():
            tell(me, (mine * 2 + d) % N_BLK)

    for t in range(2):

        @pl.when(owner(t, pair_q) != b)
        def _():
            tell(me, owner(t, pair_q))

    tell(me, after)
    tell(me, before)
    tell(me, before2)
    tell(me, next_a)
    tell(me, prev_a)
    expected = 16 * (2 - c) + 7 + 8 + 16 + 8 + 3
    expected = expected - jnp.where(yl == c, 1, 0) - jnp.where((yl == 1) & (c == 1), 1, 0)
    pl.semaphore_wait(barrier, expected)

    def column(head):
        return pl.ds(pl.multiple_of(head * HD, HD), HD)

    def piece(source, head, target, row, sems, slot, to, send_sem):
        return pltpu.make_async_remote_copy(
            src_ref=source.at[:, column(head)],
            dst_ref=target.at[pl.ds(pl.multiple_of(row, ROWS), ROWS)],
            send_sem=send_sem,
            recv_sem=sems.at[slot],
            device_id=to,
            device_id_type=MESH,
        )

    def stay(source, head, target, row, sems, slot):
        return pltpu.make_async_copy(
            source.at[:, column(head)], target.at[pl.ds(pl.multiple_of(row, ROWS), ROWS)], sems.at[slot]
        )

    key_slot, query_slot = 2 + c, (b + 1) % 2

    def scatter_a(tensor, source, target, sems, slot, to_pair):
        row = slot * BLOCK + me * ROWS

        def send(i, _):
            j = (me + 1 + i) % GROUP
            for t in range(2):
                piece(source, 3 * j + t, target, row, sems, slot, (j, owner(t, to_pair)), piece_send.at[tensor]).start()
            return 0

        lax.fori_loop(0, GROUP - 1, send, 0)
        for t in range(2):

            @pl.when(owner(t, to_pair) != b)
            def _():
                piece(source, 3 * me + t, target, row, sems, slot, (me, owner(t, to_pair)), own_send.at[tensor, t]).start()

            @pl.when(owner(t, to_pair) == b)
            def _():
                stay(source, 3 * me + t, target, row, sems, slot).start()

    def scatter_b(tensor, source, target, sems, slot, to_blk, count):
        row = slot * BLOCK + me * ROWS

        def send(i, _):
            j = (me + 1 + i) % GROUP
            piece(source, 3 * j + 2, target, row, sems, slot, (j, to_blk), piece_send.at[tensor]).start()
            return 0

        lax.fori_loop(0, count, send, 0)

    scatter_a(0, k_in, ks, k_sem, key_slot, pair)
    scatter_a(2, q_in, qs, q_sem, query_slot, pair_q)
    scatter_a(1, v_in, vs, v_sem, key_slot, pair)
    scatter_b(0, k_in, ks, k_sem, A_SLOTS + 2, b, GROUP - 1)
    stay(k_in, 3 * me + 2, ks, (A_SLOTS + 2) * BLOCK + me * ROWS, k_sem, A_SLOTS + 2).start()
    scatter_b(1, v_in, vs, v_sem, A_SLOTS + 2, b, GROUP - 1)
    stay(v_in, 3 * me + 2, vs, (A_SLOTS + 2) * BLOCK + me * ROWS, v_sem, A_SLOTS + 2).start()
    scatter_b(2, q_in, qs, q_sem, 2, before, GROUP)

    for copy in text_copies:
        copy.wait()
    for u in range(2):
        for i, target in enumerate((tks, tvs)):
            if u:
                exponent = exps[i, :, 2:3]
            else:
                exponent = jnp.where(yl == 0, exps[i, :, 0:1], exps[i, :, 1:2])
            target[u] = (codes[u, i].astype(F32) * jnp.exp2(exponent.astype(F32))).astype(BF16)
    m_s[...] = jnp.full(m_s.shape, -1e30, F32)
    acc_s[...] = jnp.zeros(acc_s.shape, F32)

    def block(ref, slot, rows=BLOCK):
        return ref.at[pl.ds(pl.multiple_of(slot * BLOCK, BLOCK), rows)]

    def arrived(ref, sems, slot):
        pltpu.make_async_copy(block(ref, slot), block(ref, slot), sems.at[slot]).wait()

    def forward(ref, sems, slot, to_slot, to_blk, send):
        return pltpu.make_async_remote_copy(
            src_ref=block(ref, slot),
            dst_ref=block(ref, to_slot),
            send_sem=fwd_send.at[send],
            recv_sem=sems.at[to_slot],
            device_id=(me, to_blk),
            device_id_type=MESH,
        )

    ONE, ZERO, THREE, TWO = A_SLOTS + 1, A_SLOTS, A_SLOTS + 3, A_SLOTS + 2
    forwards_a, forwards_even, forwards_odd, relays = [], [], [], []
    for i, (ref, sems) in enumerate(((ks, k_sem), (vs, v_sem))):
        forwards_a.append((
            forward(ref, sems, 2, 0, next_a, 7 * i),
            forward(ref, sems, 3, 1, next_a, 7 * i + 1),
            forward(ref, sems, 2, 4, prev_a, 7 * i + 2),
        ))
        forwards_even.append((
            forward(ref, sems, TWO, ZERO, after2, 7 * i + 3),
            forward(ref, sems, TWO, THREE, before, 7 * i + 4),
            forward(ref, sems, TWO, ONE, after, 7 * i + 5),
        ))
        forwards_odd.append((
            forward(ref, sems, TWO, ZERO, after2, 7 * i + 3),
            forward(ref, sems, TWO, THREE, before, 7 * i + 4),
        ))
        relays.append(forward(ref, sems, ZERO, ONE, before, 7 * i + 6))

    def pass_on_a(i, ref, sems):
        arrived(ref, sems, 2)
        forwards_a[i][0].start()
        forwards_a[i][2].start()
        arrived(ref, sems, 3)
        forwards_a[i][1].start()

    def pass_on_b(i, ref, sems):
        arrived(ref, sems, TWO)

        @pl.when(c == 0)
        def _():
            for copy in forwards_even[i]:
                copy.start()

        @pl.when(c == 1)
        def _():
            for copy in forwards_odd[i]:
                copy.start()

    def attend(query, keys, values, chunks):
        for i in range(BLOCK // TILE):
            rows = pl.ds(pl.multiple_of(query * BLOCK + i * TILE, TILE), TILE)
            q, m, acc = qs[rows, :], m_s[rows, :], acc_s[rows, :]
            for at, size in chunks:
                span = pl.ds(pl.multiple_of(at, size), size)
                k, v = keys[span, :], values[span, :]
                s = lax.dot_general(q, k, (((1,), (1,)), ((), ())), preferred_element_type=F32)
                m_new = jnp.maximum(m, jnp.max(s, axis=1, keepdims=True))
                p = jnp.exp2((s - jnp.concatenate([m_new] * (size // HD), axis=1)) * SCALE).astype(BF16)
                alpha = jnp.exp2((m - m_new) * SCALE)
                wide = jnp.concatenate([v, jnp.ones((size, HD), BF16)], axis=1)
                acc = acc * jnp.concatenate([alpha, alpha], axis=1) + jnp.dot(p, wide, preferred_element_type=F32)
                m = m_new
            m_s[rows, :] = m
            acc_s[rows, :] = acc

    def image(query, slot):
        attend(query, ks, vs, [(slot * BLOCK + n * CHUNK, CHUNK) for n in range(BLOCK // CHUNK)])

    def text(query, unit):
        attend(query, tks.at[unit], tvs.at[unit], [(0, TEXT)])

    def result(query, r, head, to_blk, send_sem):
        rows = pl.ds(pl.multiple_of(query * BLOCK + r * ROWS, ROWS), ROWS)
        return pltpu.make_async_remote_copy(
            src_ref=o_s.at[rows],
            dst_ref=out.at[:, column(head)],
            send_sem=send_sem,
            recv_sem=out_sem.at[0],
            device_id=(r, to_blk),
            device_id_type=MESH,
        )

    def finish(query, head, to_blk, count):
        rows = pl.ds(query * BLOCK, BLOCK)
        o_s[rows, :] = (acc_s[rows, :HD] / acc_s[rows, HD:]).astype(BF16)

        def send(i, _):
            result(query, (me + 1 + i) % GROUP, head, to_blk, o_send.at[query]).start()
            return 0

        lax.fori_loop(0, count, send, 0)

    def finish_a(query):
        head, to_blk = 3 * me + yl, (mine * 2 + 1 + query) % N_BLK
        finish(query, head, to_blk, GROUP - 1)

        @pl.when(to_blk != b)
        def _():
            result(query, me, head, to_blk, o_own_send.at[query]).start()

        @pl.when(to_blk == b)
        def _():
            rows = pl.ds(pl.multiple_of(query * BLOCK + me * ROWS, ROWS), ROWS)
            pltpu.make_async_copy(o_s.at[rows], out.at[:, column(head)], out_sem.at[0]).start()

    def own_blocks(query):
        def step(slot, _):
            image(query, slot)
            return 0

        lax.fori_loop(2, 4, step, 0)

    pass_on_a(0, ks, k_sem)
    arrived(qs, q_sem, 0)
    pass_on_a(1, vs, v_sem)
    own_blocks(0)
    text(0, 0)
    pass_on_b(0, ks, k_sem)
    arrived(qs, q_sem, 1)
    own_blocks(1)
    text(1, 0)
    pass_on_b(1, vs, v_sem)
    arrived(qs, q_sem, 2)
    text(2, 1)

    image(2, TWO)
    arrived(ks, k_sem, 4)
    arrived(vs, v_sem, 4)
    image(1, 4)
    arrived(ks, k_sem, THREE)
    arrived(vs, v_sem, THREE)
    image(2, THREE)
    arrived(ks, k_sem, 1)
    arrived(vs, v_sem, 1)

    def step_one(query, _):
        image(query, 1)
        return 0

    lax.fori_loop(0, 2, step_one, 0)
    finish_a(1)
    arrived(ks, k_sem, 0)
    arrived(vs, v_sem, 0)
    image(0, 0)
    finish_a(0)

    @pl.when(c == 1)
    def _():
        arrived(ks, k_sem, ZERO)
        relays[0].start()
        arrived(vs, v_sem, ZERO)
        relays[1].start()

    arrived(ks, k_sem, ONE)
    arrived(vs, v_sem, ONE)

    @pl.when(c == 0)
    def _():
        arrived(ks, k_sem, ZERO)
        arrived(vs, v_sem, ZERO)

    def step_last(slot, _):
        image(2, slot)
        return 0

    lax.fori_loop(ZERO, ONE + 1, step_last, 0)
    finish(2, 3 * me + 2, after, GROUP)

    def sent(sem, ref):
        pltpu.make_async_copy(ref, ref, sem).wait()

    sent(piece_send.at[0], ks.at[pl.ds(0, 21 * ROWS)])
    sent(piece_send.at[1], ks.at[pl.ds(0, 21 * ROWS)])
    sent(piece_send.at[2], ks.at[pl.ds(0, 22 * ROWS)])
    for tensor, to_pair in ((0, pair), (1, pair), (2, pair_q)):
        for t in range(2):

            @pl.when(owner(t, to_pair) != b)
            def _():
                sent(own_send.at[tensor, t], ks.at[pl.ds(0, ROWS)])

    for i in range(2):
        for copy in forwards_a[i]:
            copy.wait_send()

        @pl.when(c == 0)
        def _():
            for copy in forwards_even[i]:
                copy.wait_send()

        @pl.when(c == 1)
        def _():
            for copy in forwards_odd[i]:
                copy.wait_send()
            relays[i].wait_send()

    for query in range(2):
        sent(o_send.at[query], o_s.at[pl.ds(0, (GROUP - 1) * ROWS)])

        @pl.when((mine * 2 + 1 + query) % N_BLK != b)
        def _():
            sent(o_own_send.at[query], o_s.at[pl.ds(0, ROWS)])

    sent(o_send.at[2], o_s.at[pl.ds(0, GROUP * ROWS)])
    pltpu.make_async_copy(out, out, out_sem.at[0]).wait()


def local(queries, keys, values, text_codes, text_exps):
    slots = A_SLOTS + B_SLOTS
    dma = pltpu.SemaphoreType.DMA
    return pl.pallas_call(
        kernel,
        out_shape=jax.ShapeDtypeStruct(queries.shape, BF16),
        in_specs=[pl.BlockSpec(memory_space=pl.ANY)] * 5,
        out_specs=pl.BlockSpec(memory_space=pl.ANY),
        scratch_shapes=[
            pltpu.VMEM((3 * BLOCK, HD), BF16),
            pltpu.VMEM((slots * BLOCK, HD), BF16),
            pltpu.VMEM((slots * BLOCK, HD), BF16),
            pltpu.VMEM((2, TEXT, HD), BF16),
            pltpu.VMEM((2, TEXT, HD), BF16),
            pltpu.VMEM((2, 2, TEXT, HD), jnp.int32),
            pltpu.VMEM(text_exps.shape, jnp.int32),
            pltpu.VMEM((3 * BLOCK, HD), F32),
            pltpu.VMEM((3 * BLOCK, 2 * HD), F32),
            pltpu.VMEM((3 * BLOCK, HD), BF16),
            dma((3,)),
            dma((slots,)),
            dma((slots,)),
            dma((3,)),
            dma((1,)),
            dma((3,)),
            dma((3, 2)),
            dma((14,)),
            dma((3,)),
            dma((2,)),
        ],
        compiler_params=pltpu.CompilerParams(collective_id=0, has_side_effects=True, vmem_limit_bytes=50 << 20),
        cost_estimate=pl.CostEstimate(flops=7 * 10**9, bytes_accessed=4 * 10**6, transcendentals=14 * 10**6),
    )(queries, keys, values, text_codes, text_exps)


def solution(mesh):
    rows = P(("blk", "head"), None)
    text = P(None, None, "head")
    return jax.shard_map(
        local, mesh=mesh, in_specs=(rows, rows, rows, text, text), out_specs=rows, check_vma=False
    )
```

```python
import math

import jax
import jax.numpy as jnp
from jax import lax
from jax.experimental import pallas as pl
from jax.experimental.pallas import tpu as pltpu
from jax.sharding import PartitionSpec as P

HD = 128
ROWS = 128
BLOCK = 1024
TEXT = 256
GROUP = 8
N_BLK = 32
PAIRS = 16
A_SLOTS, B_SLOTS = 5, 4
TILE = 256
CHUNK = 512
MESH = pl.DeviceIdType.MESH
SCALE = math.log2(math.e) / math.sqrt(HD)
BF16, F32 = jnp.bfloat16, jnp.float32


def owner(t, p):
    return (t * 8 + p % 8) * 2 + p // 8


def kernel(
    q_in, k_in, v_in, codes_in, exps_in, out,
    qs, ks, vs, tks, tvs, codes, exps, m_s, acc_s, o_s,
    text_sem, k_sem, v_sem, q_sem, out_sem,
    piece_send, own_send, fwd_send, o_send, o_own_send,
):
    me = lax.axis_index("head")
    b = lax.axis_index("blk")
    yl, z, c = b // 16, (b // 2) % 8, b % 2
    pair, pair_q = b // 2, ((b + N_BLK - 1) % N_BLK) // 2
    mine = c * 8 + z
    after, after2 = (b + 1) % N_BLK, (b + 2) % N_BLK
    before, before2 = (b + N_BLK - 1) % N_BLK, (b + N_BLK - 2) % N_BLK
    next_a, prev_a = owner(yl, (mine + 1) % PAIRS), owner(yl, (mine + PAIRS - 1) % PAIRS)

    text_copies = [
        pltpu.make_async_copy(codes_in.at[:, :, pl.ds(pl.multiple_of(yl * HD, HD), HD)], codes.at[0], text_sem.at[0]),
        pltpu.make_async_copy(codes_in.at[:, :, pl.ds(2 * HD, HD)], codes.at[1], text_sem.at[1]),
        pltpu.make_async_copy(exps_in, exps, text_sem.at[2]),
    ]
    for copy in text_copies:
        copy.start()

    barrier = pltpu.get_barrier_semaphore()

    def tell(head, blk):
        pl.semaphore_signal(barrier, inc=1, device_id=(head, blk), device_id_type=MESH)

    def greet(i, _):
        other = (me + 1 + i) % GROUP
        for d in range(3):
            tell(other, (mine * 2 + d) % N_BLK)
        tell(other, b)
        tell(other, after)
        tell(other, before)
        for t in range(2):
            tell(other, owner(t, pair_q))
        return 0

    lax.fori_loop(0, GROUP - 1, greet, 0)
    for d in range(3):

        @pl.when((mine * 2 + d) % N_BLK != b)
        def _():
            tell(me, (mine * 2 + d) % N_BLK)

    for t in range(2):

        @pl.when(owner(t, pair_q) != b)
        def _():
            tell(me, owner(t, pair_q))

    tell(me, after)
    tell(me, before)
    tell(me, before2)
    tell(me, next_a)
    tell(me, prev_a)
    expected = 16 * (2 - c) + 7 + 8 + 16 + 8 + 3
    expected = expected - jnp.where(yl == c, 1, 0) - jnp.where((yl == 1) & (c == 1), 1, 0)
    pl.semaphore_wait(barrier, expected)

    def column(head):
        return pl.ds(pl.multiple_of(head * HD, HD), HD)

    def piece(source, head, target, row, sems, slot, to, send_sem):
        return pltpu.make_async_remote_copy(
            src_ref=source.at[:, column(head)],
            dst_ref=target.at[pl.ds(pl.multiple_of(row, ROWS), ROWS)],
            send_sem=send_sem,
            recv_sem=sems.at[slot],
            device_id=to,
            device_id_type=MESH,
        )

    def stay(source, head, target, row, sems, slot):
        return pltpu.make_async_copy(
            source.at[:, column(head)], target.at[pl.ds(pl.multiple_of(row, ROWS), ROWS)], sems.at[slot]
        )

    key_slot, query_slot = 2 + c, (b + 1) % 2

    def scatter_a(tensor, source, target, sems, slot, to_pair):
        row = slot * BLOCK + me * ROWS

        def send(i, _):
            j = (me + 1 + i) % GROUP
            for t in range(2):
                piece(source, 3 * j + t, target, row, sems, slot, (j, owner(t, to_pair)), piece_send.at[tensor]).start()
            return 0

        lax.fori_loop(0, GROUP - 1, send, 0)
        for t in range(2):

            @pl.when(owner(t, to_pair) != b)
            def _():
                piece(source, 3 * me + t, target, row, sems, slot, (me, owner(t, to_pair)), own_send.at[tensor, t]).start()

            @pl.when(owner(t, to_pair) == b)
            def _():
                stay(source, 3 * me + t, target, row, sems, slot).start()

    def scatter_b(tensor, source, target, sems, slot, to_blk, count):
        row = slot * BLOCK + me * ROWS

        def send(i, _):
            j = (me + 1 + i) % GROUP
            piece(source, 3 * j + 2, target, row, sems, slot, (j, to_blk), piece_send.at[tensor]).start()
            return 0

        lax.fori_loop(0, count, send, 0)

    scatter_a(0, k_in, ks, k_sem, key_slot, pair)
    scatter_a(1, v_in, vs, v_sem, key_slot, pair)
    for copy in text_copies:
        copy.wait()
    for u in range(2):
        for i, target in enumerate((tks, tvs)):
            if u:
                exponent = exps[2, i : i + 1, :]
            else:
                exponent = jnp.where(yl == 0, exps[0, i : i + 1, :], exps[1, i : i + 1, :])
            scales = jnp.broadcast_to(jnp.exp2(exponent.astype(F32)), (HD, TEXT)).T
            target[u] = (codes[u, i].astype(F32) * scales).astype(BF16)
    m_s[...] = jnp.full(m_s.shape, -1e30, F32)
    acc_s[...] = jnp.zeros(acc_s.shape, F32)

    def block(ref, slot, rows=BLOCK):
        return ref.at[pl.ds(pl.multiple_of(slot * BLOCK, BLOCK), rows)]

    def arrived(ref, sems, slot):
        pltpu.make_async_copy(block(ref, slot), block(ref, slot), sems.at[slot]).wait()

    def forward(ref, sems, slot, to_slot, to_blk, send):
        return pltpu.make_async_remote_copy(
            src_ref=block(ref, slot),
            dst_ref=block(ref, to_slot),
            send_sem=fwd_send.at[send],
            recv_sem=sems.at[to_slot],
            device_id=(me, to_blk),
            device_id_type=MESH,
        )

    ONE, ZERO, THREE, TWO = A_SLOTS + 1, A_SLOTS, A_SLOTS + 3, A_SLOTS + 2
    forwards_a, forwards_even, forwards_odd, relays = [], [], [], []
    for i, (ref, sems) in enumerate(((ks, k_sem), (vs, v_sem))):
        forwards_a.append((
            forward(ref, sems, 2, 0, next_a, 7 * i),
            forward(ref, sems, 3, 1, next_a, 7 * i + 1),
            forward(ref, sems, 2, 4, prev_a, 7 * i + 2),
        ))
        forwards_even.append((
            forward(ref, sems, TWO, ZERO, after2, 7 * i + 3),
            forward(ref, sems, TWO, THREE, before, 7 * i + 4),
            forward(ref, sems, TWO, ONE, after, 7 * i + 5),
        ))
        forwards_odd.append((
            forward(ref, sems, TWO, ZERO, after2, 7 * i + 3),
            forward(ref, sems, TWO, THREE, before, 7 * i + 4),
        ))
        relays.append(forward(ref, sems, ZERO, ONE, before, 7 * i + 6))

    def pass_on_a(i, ref, sems):
        arrived(ref, sems, 2)
        forwards_a[i][0].start()
        forwards_a[i][2].start()
        arrived(ref, sems, 3)
        forwards_a[i][1].start()

    def pass_on_b(i, ref, sems):
        arrived(ref, sems, TWO)

        @pl.when(c == 0)
        def _():
            for copy in forwards_even[i]:
                copy.start()

        @pl.when(c == 1)
        def _():
            for copy in forwards_odd[i]:
                copy.start()

    def attend(query, keys, values, chunks):
        for i in range(BLOCK // TILE):
            rows = pl.ds(pl.multiple_of(query * BLOCK + i * TILE, TILE), TILE)
            q, m, acc = qs[rows, :], m_s[rows, :], acc_s[rows, :]
            for at, size in chunks:
                span = pl.ds(pl.multiple_of(at, size), size)
                k, v = keys[span, :], values[span, :]
                s = lax.dot_general(q, k, (((1,), (1,)), ((), ())), preferred_element_type=F32)
                m_new = jnp.maximum(m, jnp.max(s, axis=1, keepdims=True))
                p = jnp.exp2((s - jnp.concatenate([m_new] * (size // HD), axis=1)) * SCALE).astype(BF16)
                alpha = jnp.exp2((m - m_new) * SCALE)
                wide = jnp.concatenate([v, jnp.ones((size, HD), BF16)], axis=1)
                acc = acc * jnp.concatenate([alpha, alpha], axis=1) + jnp.dot(p, wide, preferred_element_type=F32)
                m = m_new
            m_s[rows, :] = m
            acc_s[rows, :] = acc

    def image(query, slot):
        attend(query, ks, vs, [(slot * BLOCK + n * CHUNK, CHUNK) for n in range(BLOCK // CHUNK)])

    def text(query, unit):
        attend(query, tks.at[unit], tvs.at[unit], [(0, TEXT)])

    def result(query, r, head, to_blk, send_sem):
        rows = pl.ds(pl.multiple_of(query * BLOCK + r * ROWS, ROWS), ROWS)
        return pltpu.make_async_remote_copy(
            src_ref=o_s.at[rows],
            dst_ref=out.at[:, column(head)],
            send_sem=send_sem,
            recv_sem=out_sem.at[0],
            device_id=(r, to_blk),
            device_id_type=MESH,
        )

    def finish(query, head, to_blk, count):
        rows = pl.ds(query * BLOCK, BLOCK)
        o_s[rows, :] = (acc_s[rows, :HD] / acc_s[rows, HD:]).astype(BF16)

        def send(i, _):
            result(query, (me + 1 + i) % GROUP, head, to_blk, o_send.at[query]).start()
            return 0

        lax.fori_loop(0, count, send, 0)

    def finish_a(query):
        head, to_blk = 3 * me + yl, (mine * 2 + 1 + query) % N_BLK
        finish(query, head, to_blk, GROUP - 1)

        @pl.when(to_blk != b)
        def _():
            result(query, me, head, to_blk, o_own_send.at[query]).start()

        @pl.when(to_blk == b)
        def _():
            rows = pl.ds(pl.multiple_of(query * BLOCK + me * ROWS, ROWS), ROWS)
            pltpu.make_async_copy(o_s.at[rows], out.at[:, column(head)], out_sem.at[0]).start()

    def own_blocks(query):
        def step(slot, _):
            image(query, slot)
            return 0

        lax.fori_loop(2, 4, step, 0)

    pass_on_a(0, ks, k_sem)
    scatter_a(2, q_in, qs, q_sem, query_slot, pair_q)
    pass_on_a(1, vs, v_sem)
    scatter_b(0, k_in, ks, k_sem, A_SLOTS + 2, b, GROUP - 1)
    stay(k_in, 3 * me + 2, ks, (A_SLOTS + 2) * BLOCK + me * ROWS, k_sem, A_SLOTS + 2).start()
    scatter_b(1, v_in, vs, v_sem, A_SLOTS + 2, b, GROUP - 1)
    stay(v_in, 3 * me + 2, vs, (A_SLOTS + 2) * BLOCK + me * ROWS, v_sem, A_SLOTS + 2).start()
    scatter_b(2, q_in, qs, q_sem, 2, before, GROUP)
    arrived(qs, q_sem, 0)
    own_blocks(0)
    text(0, 0)
    pass_on_b(0, ks, k_sem)
    arrived(qs, q_sem, 1)
    own_blocks(1)
    text(1, 0)
    pass_on_b(1, vs, v_sem)
    arrived(qs, q_sem, 2)
    text(2, 1)

    image(2, TWO)
    arrived(ks, k_sem, 4)
    arrived(vs, v_sem, 4)
    image(1, 4)
    arrived(ks, k_sem, THREE)
    arrived(vs, v_sem, THREE)
    image(2, THREE)
    arrived(ks, k_sem, 1)
    arrived(vs, v_sem, 1)

    def step_one(query, _):
        image(query, 1)
        return 0

    lax.fori_loop(0, 2, step_one, 0)
    finish_a(1)
    arrived(ks, k_sem, 0)
    arrived(vs, v_sem, 0)
    image(0, 0)
    finish_a(0)

    @pl.when(c == 1)
    def _():
        arrived(ks, k_sem, ZERO)
        relays[0].start()
        arrived(vs, v_sem, ZERO)
        relays[1].start()

    arrived(ks, k_sem, ONE)
    arrived(vs, v_sem, ONE)

    @pl.when(c == 0)
    def _():
        arrived(ks, k_sem, ZERO)
        arrived(vs, v_sem, ZERO)

    def step_last(slot, _):
        image(2, slot)
        return 0

    lax.fori_loop(ZERO, ONE + 1, step_last, 0)
    finish(2, 3 * me + 2, after, GROUP)

    def sent(sem, ref):
        pltpu.make_async_copy(ref, ref, sem).wait()

    sent(piece_send.at[0], ks.at[pl.ds(0, 21 * ROWS)])
    sent(piece_send.at[1], ks.at[pl.ds(0, 21 * ROWS)])
    sent(piece_send.at[2], ks.at[pl.ds(0, 22 * ROWS)])
    for tensor, to_pair in ((0, pair), (1, pair), (2, pair_q)):
        for t in range(2):

            @pl.when(owner(t, to_pair) != b)
            def _():
                sent(own_send.at[tensor, t], ks.at[pl.ds(0, ROWS)])

    for i in range(2):
        for copy in forwards_a[i]:
            copy.wait_send()

        @pl.when(c == 0)
        def _():
            for copy in forwards_even[i]:
                copy.wait_send()

        @pl.when(c == 1)
        def _():
            for copy in forwards_odd[i]:
                copy.wait_send()
            relays[i].wait_send()

    for query in range(2):
        sent(o_send.at[query], o_s.at[pl.ds(0, (GROUP - 1) * ROWS)])

        @pl.when((mine * 2 + 1 + query) % N_BLK != b)
        def _():
            sent(o_own_send.at[query], o_s.at[pl.ds(0, ROWS)])

    sent(o_send.at[2], o_s.at[pl.ds(0, GROUP * ROWS)])
    pltpu.make_async_copy(out, out, out_sem.at[0]).wait()


def local(queries, keys, values, text_codes, text_exps):
    slots = A_SLOTS + B_SLOTS
    dma = pltpu.SemaphoreType.DMA
    return pl.pallas_call(
        kernel,
        out_shape=jax.ShapeDtypeStruct(queries.shape, BF16),
        in_specs=[pl.BlockSpec(memory_space=pl.ANY)] * 5,
        out_specs=pl.BlockSpec(memory_space=pl.ANY),
        scratch_shapes=[
            pltpu.VMEM((3 * BLOCK, HD), BF16),
            pltpu.VMEM((slots * BLOCK, HD), BF16),
            pltpu.VMEM((slots * BLOCK, HD), BF16),
            pltpu.VMEM((2, TEXT, HD), BF16),
            pltpu.VMEM((2, TEXT, HD), BF16),
            pltpu.VMEM((2, 2, TEXT, HD), jnp.int32),
            pltpu.VMEM((3, 2, TEXT), jnp.int32),
            pltpu.VMEM((3 * BLOCK, HD), F32),
            pltpu.VMEM((3 * BLOCK, 2 * HD), F32),
            pltpu.VMEM((3 * BLOCK, HD), BF16),
            dma((3,)),
            dma((slots,)),
            dma((slots,)),
            dma((3,)),
            dma((1,)),
            dma((3,)),
            dma((3, 2)),
            dma((14,)),
            dma((3,)),
            dma((2,)),
        ],
        compiler_params=pltpu.CompilerParams(collective_id=0, has_side_effects=True, vmem_limit_bytes=63 << 20),
        cost_estimate=pl.CostEstimate(flops=7 * 10**9, bytes_accessed=4 * 10**6, transcendentals=14 * 10**6),
    )(queries, keys, values, text_codes, jnp.transpose(text_exps, (2, 0, 1)))


def solution(mesh):
    rows = P(("blk", "head"), None)
    text = P(None, None, "head")
    return jax.shard_map(
        local, mesh=mesh, in_specs=(rows, rows, rows, text, text), out_specs=rows, check_vma=False
    )
```

```python
import math

import jax
import jax.numpy as jnp
from jax import lax
from jax.experimental import pallas as pl
from jax.experimental.pallas import tpu as pltpu
from jax.sharding import PartitionSpec as P

HD = 128
ROWS = 128
BLOCK = 1024
TEXT = 256
GROUP = 8
N_BLK = 32
PAIRS = 16
A_SLOTS, B_SLOTS = 5, 4
TILE = 256
CHUNK = 512
MESH = pl.DeviceIdType.MESH
SCALE = math.log2(math.e) / math.sqrt(HD)
BF16, F32 = jnp.bfloat16, jnp.float32


def owner(t, p):
    return (t * 8 + p % 8) * 2 + p // 8


def kernel(
    q_in, k_in, v_in, codes_in, exps_in, out,
    qs, ks, vs, tks, tvs, codes, exps, m_s, acc_s, o_s,
    text_sem, k_sem, v_sem, q_sem, out_sem,
    piece_send, own_send, fwd_send, o_send, o_own_send,
):
    me = lax.axis_index("head")
    b = lax.axis_index("blk")
    yl, z, c = b // 16, (b // 2) % 8, b % 2
    pair, pair_q = b // 2, ((b + N_BLK - 1) % N_BLK) // 2
    mine = c * 8 + z
    after, after2 = (b + 1) % N_BLK, (b + 2) % N_BLK
    before, before2 = (b + N_BLK - 1) % N_BLK, (b + N_BLK - 2) % N_BLK
    next_a, prev_a = owner(yl, (mine + 1) % PAIRS), owner(yl, (mine + PAIRS - 1) % PAIRS)

    text_copies = [
        pltpu.make_async_copy(codes_in.at[:, :, pl.ds(pl.multiple_of(yl * HD, HD), HD)], codes.at[0], text_sem.at[0]),
        pltpu.make_async_copy(codes_in.at[:, :, pl.ds(2 * HD, HD)], codes.at[1], text_sem.at[1]),
        pltpu.make_async_copy(exps_in, exps, text_sem.at[2]),
    ]
    for copy in text_copies:
        copy.start()

    barrier = pltpu.get_barrier_semaphore()

    def tell(head, blk):
        pl.semaphore_signal(barrier, inc=1, device_id=(head, blk), device_id_type=MESH)

    def greet(i, _):
        other = (me + 1 + i) % GROUP
        for d in range(3):
            tell(other, (mine * 2 + d) % N_BLK)
        tell(other, b)
        tell(other, after)
        tell(other, before)
        for t in range(2):
            tell(other, owner(t, pair_q))
        return 0

    lax.fori_loop(0, GROUP - 1, greet, 0)
    for d in range(3):

        @pl.when((mine * 2 + d) % N_BLK != b)
        def _():
            tell(me, (mine * 2 + d) % N_BLK)

    for t in range(2):

        @pl.when(owner(t, pair_q) != b)
        def _():
            tell(me, owner(t, pair_q))

    tell(me, after)
    tell(me, before)
    tell(me, before2)
    tell(me, next_a)
    tell(me, prev_a)
    expected = 16 * (2 - c) + 7 + 8 + 16 + 8 + 3
    expected = expected - jnp.where(yl == c, 1, 0) - jnp.where((yl == 1) & (c == 1), 1, 0)
    pl.semaphore_wait(barrier, expected)

    def column(head):
        return pl.ds(pl.multiple_of(head * HD, HD), HD)

    def piece(source, head, target, row, sems, slot, to, send_sem):
        return pltpu.make_async_remote_copy(
            src_ref=source.at[:, column(head)],
            dst_ref=target.at[pl.ds(pl.multiple_of(row, ROWS), ROWS)],
            send_sem=send_sem,
            recv_sem=sems.at[slot],
            device_id=to,
            device_id_type=MESH,
        )

    def stay(source, head, target, row, sems, slot):
        return pltpu.make_async_copy(
            source.at[:, column(head)], target.at[pl.ds(pl.multiple_of(row, ROWS), ROWS)], sems.at[slot]
        )

    key_slot, query_slot = 2 + c, (b + 1) % 2

    def scatter_a(tensor, source, target, sems, slot, to_pair):
        row = slot * BLOCK + me * ROWS

        def send(i, _):
            j = (me + 1 + i) % GROUP
            for t in range(2):
                piece(source, 3 * j + t, target, row, sems, slot, (j, owner(t, to_pair)), piece_send.at[tensor]).start()
            return 0

        lax.fori_loop(0, GROUP - 1, send, 0)
        for t in range(2):

            @pl.when(owner(t, to_pair) != b)
            def _():
                piece(source, 3 * me + t, target, row, sems, slot, (me, owner(t, to_pair)), own_send.at[tensor, t]).start()

            @pl.when(owner(t, to_pair) == b)
            def _():
                stay(source, 3 * me + t, target, row, sems, slot).start()

    def scatter_b(tensor, source, target, sems, slot, to_blk, count):
        row = slot * BLOCK + me * ROWS

        def send(i, _):
            j = (me + 1 + i) % GROUP
            piece(source, 3 * j + 2, target, row, sems, slot, (j, to_blk), piece_send.at[tensor]).start()
            return 0

        lax.fori_loop(0, count, send, 0)

    scatter_a(0, k_in, ks, k_sem, key_slot, pair)
    scatter_a(1, v_in, vs, v_sem, key_slot, pair)
    for copy in text_copies:
        copy.wait()
    for u in range(2):
        for i, target in enumerate((tks, tvs)):
            if u:
                exponent = exps[2, i : i + 1, :]
            else:
                exponent = jnp.where(yl == 0, exps[0, i : i + 1, :], exps[1, i : i + 1, :])
            scales = jnp.broadcast_to(jnp.exp2(exponent.astype(F32)), (HD, TEXT)).T
            target[u] = (codes[u, i].astype(F32) * scales).astype(BF16)
    m_s[...] = jnp.full(m_s.shape, -1e30, F32)
    acc_s[...] = jnp.zeros(acc_s.shape, F32)

    def block(ref, slot, rows=BLOCK):
        return ref.at[pl.ds(pl.multiple_of(slot * BLOCK, BLOCK), rows)]

    def arrived(ref, sems, slot):
        pltpu.make_async_copy(block(ref, slot), block(ref, slot), sems.at[slot]).wait()

    def forward(ref, sems, slot, to_slot, to_blk, send):
        return pltpu.make_async_remote_copy(
            src_ref=block(ref, slot),
            dst_ref=block(ref, to_slot),
            send_sem=fwd_send.at[send],
            recv_sem=sems.at[to_slot],
            device_id=(me, to_blk),
            device_id_type=MESH,
        )

    ONE, ZERO, THREE, TWO = A_SLOTS + 1, A_SLOTS, A_SLOTS + 3, A_SLOTS + 2
    forwards_a, forwards_even, forwards_odd, relays = [], [], [], []
    for i, (ref, sems) in enumerate(((ks, k_sem), (vs, v_sem))):
        forwards_a.append((
            forward(ref, sems, 2, 0, next_a, 7 * i),
            forward(ref, sems, 3, 1, next_a, 7 * i + 1),
            forward(ref, sems, 2, 4, prev_a, 7 * i + 2),
        ))
        forwards_even.append((
            forward(ref, sems, TWO, ZERO, after2, 7 * i + 3),
            forward(ref, sems, TWO, THREE, before, 7 * i + 4),
            forward(ref, sems, TWO, ONE, after, 7 * i + 5),
        ))
        forwards_odd.append((
            forward(ref, sems, TWO, ZERO, after2, 7 * i + 3),
            forward(ref, sems, TWO, THREE, before, 7 * i + 4),
        ))
        relays.append(forward(ref, sems, ZERO, ONE, before, 7 * i + 6))

    def pass_on_a(i, ref, sems):
        arrived(ref, sems, 2)
        forwards_a[i][0].start()
        forwards_a[i][2].start()
        arrived(ref, sems, 3)
        forwards_a[i][1].start()

    def pass_on_b(i, ref, sems):
        arrived(ref, sems, TWO)
        forwards_a[i][0].wait_send()
        forwards_a[i][1].wait_send()

        @pl.when(c == 0)
        def _():
            for copy in forwards_even[i]:
                copy.start()

        @pl.when(c == 1)
        def _():
            for copy in forwards_odd[i]:
                copy.start()

    def attend(query, keys, values, chunks):
        for i in range(BLOCK // TILE):
            rows = pl.ds(pl.multiple_of(query * BLOCK + i * TILE, TILE), TILE)
            q, m, acc = qs[rows, :], m_s[rows, :], acc_s[rows, :]
            for at, size in chunks:
                span = pl.ds(pl.multiple_of(at, size), size)
                k, v = keys[span, :], values[span, :]
                s = lax.dot_general(q, k, (((1,), (1,)), ((), ())), preferred_element_type=F32)
                m_new = jnp.maximum(m, jnp.max(s, axis=1, keepdims=True))
                p = jnp.exp2((s - jnp.concatenate([m_new] * (size // HD), axis=1)) * SCALE).astype(BF16)
                alpha = jnp.exp2((m - m_new) * SCALE)
                wide = jnp.concatenate([v, jnp.ones((size, HD), BF16)], axis=1)
                acc = acc * jnp.concatenate([alpha, alpha], axis=1) + jnp.dot(p, wide, preferred_element_type=F32)
                m = m_new
            m_s[rows, :] = m
            acc_s[rows, :] = acc

    def image(query, slot):
        attend(query, ks, vs, [(slot * BLOCK + n * CHUNK, CHUNK) for n in range(BLOCK // CHUNK)])

    def text(query, unit):
        attend(query, tks.at[unit], tvs.at[unit], [(0, TEXT)])

    def result(query, r, head, to_blk, send_sem):
        rows = pl.ds(pl.multiple_of(query * BLOCK + r * ROWS, ROWS), ROWS)
        return pltpu.make_async_remote_copy(
            src_ref=o_s.at[rows],
            dst_ref=out.at[:, column(head)],
            send_sem=send_sem,
            recv_sem=out_sem.at[0],
            device_id=(r, to_blk),
            device_id_type=MESH,
        )

    def finish(query, head, to_blk, count):
        rows = pl.ds(query * BLOCK, BLOCK)
        o_s[rows, :] = (acc_s[rows, :HD] / acc_s[rows, HD:]).astype(BF16)

        def send(i, _):
            result(query, (me + 1 + i) % GROUP, head, to_blk, o_send.at[query]).start()
            return 0

        lax.fori_loop(0, count, send, 0)

    def finish_a(query):
        head, to_blk = 3 * me + yl, (mine * 2 + 1 + query) % N_BLK
        finish(query, head, to_blk, GROUP - 1)

        @pl.when(to_blk != b)
        def _():
            result(query, me, head, to_blk, o_own_send.at[query]).start()

        @pl.when(to_blk == b)
        def _():
            rows = pl.ds(pl.multiple_of(query * BLOCK + me * ROWS, ROWS), ROWS)
            pltpu.make_async_copy(o_s.at[rows], out.at[:, column(head)], out_sem.at[0]).start()

    def own_blocks(query):
        def step(slot, _):
            image(query, slot)
            return 0

        lax.fori_loop(2, 4, step, 0)

    pass_on_a(0, ks, k_sem)
    scatter_a(2, q_in, qs, q_sem, query_slot, pair_q)
    pass_on_a(1, vs, v_sem)
    scatter_b(0, k_in, ks, k_sem, A_SLOTS + 2, b, GROUP - 1)
    stay(k_in, 3 * me + 2, ks, (A_SLOTS + 2) * BLOCK + me * ROWS, k_sem, A_SLOTS + 2).start()
    scatter_b(1, v_in, vs, v_sem, A_SLOTS + 2, b, GROUP - 1)
    stay(v_in, 3 * me + 2, vs, (A_SLOTS + 2) * BLOCK + me * ROWS, v_sem, A_SLOTS + 2).start()
    scatter_b(2, q_in, qs, q_sem, 2, before, GROUP)
    arrived(qs, q_sem, 0)
    own_blocks(0)
    text(0, 0)
    pass_on_b(0, ks, k_sem)
    arrived(qs, q_sem, 1)
    own_blocks(1)
    text(1, 0)
    pass_on_b(1, vs, v_sem)
    arrived(qs, q_sem, 2)
    text(2, 1)

    image(2, TWO)
    arrived(ks, k_sem, 4)
    arrived(vs, v_sem, 4)
    image(1, 4)
    arrived(ks, k_sem, THREE)
    arrived(vs, v_sem, THREE)
    image(2, THREE)
    arrived(ks, k_sem, 1)
    arrived(vs, v_sem, 1)

    def step_one(query, _):
        image(query, 1)
        return 0

    lax.fori_loop(0, 2, step_one, 0)
    finish_a(1)
    arrived(ks, k_sem, 0)
    arrived(vs, v_sem, 0)
    image(0, 0)
    finish_a(0)

    @pl.when(c == 1)
    def _():
        arrived(ks, k_sem, ZERO)
        relays[0].start()
        arrived(vs, v_sem, ZERO)
        relays[1].start()

    arrived(ks, k_sem, ONE)
    arrived(vs, v_sem, ONE)

    @pl.when(c == 0)
    def _():
        arrived(ks, k_sem, ZERO)
        arrived(vs, v_sem, ZERO)

    def step_last(slot, _):
        image(2, slot)
        return 0

    lax.fori_loop(ZERO, ONE + 1, step_last, 0)
    finish(2, 3 * me + 2, after, GROUP)

    def sent(sem, ref):
        pltpu.make_async_copy(ref, ref, sem).wait()

    sent(piece_send.at[0], ks.at[pl.ds(0, 21 * ROWS)])
    sent(piece_send.at[1], ks.at[pl.ds(0, 21 * ROWS)])
    sent(piece_send.at[2], ks.at[pl.ds(0, 22 * ROWS)])
    for tensor, to_pair in ((0, pair), (1, pair), (2, pair_q)):
        for t in range(2):

            @pl.when(owner(t, to_pair) != b)
            def _():
                sent(own_send.at[tensor, t], ks.at[pl.ds(0, ROWS)])

    for i in range(2):
        forwards_a[i][2].wait_send()

        @pl.when(c == 0)
        def _():
            for copy in forwards_even[i]:
                copy.wait_send()

        @pl.when(c == 1)
        def _():
            for copy in forwards_odd[i]:
                copy.wait_send()
            relays[i].wait_send()

    for query in range(2):
        sent(o_send.at[query], o_s.at[pl.ds(0, (GROUP - 1) * ROWS)])

        @pl.when((mine * 2 + 1 + query) % N_BLK != b)
        def _():
            sent(o_own_send.at[query], o_s.at[pl.ds(0, ROWS)])

    sent(o_send.at[2], o_s.at[pl.ds(0, GROUP * ROWS)])
    pltpu.make_async_copy(out, out, out_sem.at[0]).wait()


def local(queries, keys, values, text_codes, text_exps):
    slots = A_SLOTS + B_SLOTS
    dma = pltpu.SemaphoreType.DMA
    return pl.pallas_call(
        kernel,
        out_shape=jax.ShapeDtypeStruct(queries.shape, BF16),
        in_specs=[pl.BlockSpec(memory_space=pl.ANY)] * 5,
        out_specs=pl.BlockSpec(memory_space=pl.ANY),
        scratch_shapes=[
            pltpu.VMEM((3 * BLOCK, HD), BF16),
            pltpu.VMEM((slots * BLOCK, HD), BF16),
            pltpu.VMEM((slots * BLOCK, HD), BF16),
            pltpu.VMEM((2, TEXT, HD), BF16),
            pltpu.VMEM((2, TEXT, HD), BF16),
            pltpu.VMEM((2, 2, TEXT, HD), jnp.int32),
            pltpu.VMEM((3, 2, TEXT), jnp.int32),
            pltpu.VMEM((3 * BLOCK, HD), F32),
            pltpu.VMEM((3 * BLOCK, 2 * HD), F32),
            pltpu.VMEM((3 * BLOCK, HD), BF16),
            dma((3,)),
            dma((slots,)),
            dma((slots,)),
            dma((3,)),
            dma((1,)),
            dma((3,)),
            dma((3, 2)),
            dma((14,)),
            dma((3,)),
            dma((2,)),
        ],
        compiler_params=pltpu.CompilerParams(collective_id=0, has_side_effects=True, vmem_limit_bytes=63 << 20),
        cost_estimate=pl.CostEstimate(flops=7 * 10**9, bytes_accessed=4 * 10**6, transcendentals=14 * 10**6),
    )(queries, keys, values, text_codes, jnp.transpose(text_exps, (2, 0, 1)))


def solution(mesh):
    rows = P(("blk", "head"), None)
    text = P(None, None, "head")
    return jax.shard_map(
        local, mesh=mesh, in_specs=(rows, rows, rows, text, text), out_specs=rows, check_vma=False
    )
```

```python
import math

import jax
import jax.numpy as jnp
from jax import lax
from jax.experimental import pallas as pl
from jax.experimental.pallas import tpu as pltpu
from jax.sharding import PartitionSpec as P

HD = 128
ROWS = 128
BLOCK = 1024
TEXT = 256
GROUP = 8
N_BLK = 32
PAIRS = 16
A_SLOTS, B_SLOTS = 5, 4
TILE = 256
CHUNK = 512
MESH = pl.DeviceIdType.MESH
SCALE = math.log2(math.e) / math.sqrt(HD)
BF16, F32 = jnp.bfloat16, jnp.float32


def owner(t, p):
    return (t * 8 + p % 8) * 2 + p // 8


def kernel(
    q_in, k_in, v_in, codes_in, exps_in, out,
    qs, ks, vs, tks, tvs, codes, exps, m_s, acc_s, o_s,
    text_sem, k_sem, v_sem, q_sem, out_sem,
    piece_send, own_send, fwd_send, o_send, o_own_send,
):
    me = lax.axis_index("head")
    b = lax.axis_index("blk")
    yl, z, c = b // 16, (b // 2) % 8, b % 2
    pair, pair_q = b // 2, ((b + N_BLK - 1) % N_BLK) // 2
    mine = c * 8 + z
    after, after2 = (b + 1) % N_BLK, (b + 2) % N_BLK
    before, before2 = (b + N_BLK - 1) % N_BLK, (b + N_BLK - 2) % N_BLK
    next_a, prev_a = owner(yl, (mine + 1) % PAIRS), owner(yl, (mine + PAIRS - 1) % PAIRS)

    text_copies = [
        pltpu.make_async_copy(codes_in.at[:, :, pl.ds(pl.multiple_of(yl * HD, HD), HD)], codes.at[0], text_sem.at[0]),
        pltpu.make_async_copy(codes_in.at[:, :, pl.ds(2 * HD, HD)], codes.at[1], text_sem.at[1]),
        pltpu.make_async_copy(exps_in, exps, text_sem.at[2]),
    ]
    for copy in text_copies:
        copy.start()

    barrier = pltpu.get_barrier_semaphore()

    def tell(head, blk):
        pl.semaphore_signal(barrier, inc=1, device_id=(head, blk), device_id_type=MESH)

    def greet(i, _):
        other = (me + 1 + i) % GROUP
        for d in range(3):
            tell(other, (mine * 2 + d) % N_BLK)
        tell(other, b)
        tell(other, after)
        tell(other, before)
        for t in range(2):
            tell(other, owner(t, pair_q))
        return 0

    lax.fori_loop(0, GROUP - 1, greet, 0)
    for d in range(3):

        @pl.when((mine * 2 + d) % N_BLK != b)
        def _():
            tell(me, (mine * 2 + d) % N_BLK)

    for t in range(2):

        @pl.when(owner(t, pair_q) != b)
        def _():
            tell(me, owner(t, pair_q))

    tell(me, after)
    tell(me, before)
    tell(me, before2)
    tell(me, next_a)
    tell(me, prev_a)
    expected = 16 * (2 - c) + 7 + 8 + 16 + 8 + 3
    expected = expected - jnp.where(yl == c, 1, 0) - jnp.where((yl == 1) & (c == 1), 1, 0)
    pl.semaphore_wait(barrier, expected)

    def column(head):
        return pl.ds(pl.multiple_of(head * HD, HD), HD)

    def piece(source, head, target, row, sems, slot, to, send_sem):
        return pltpu.make_async_remote_copy(
            src_ref=source.at[:, column(head)],
            dst_ref=target.at[pl.ds(pl.multiple_of(row, ROWS), ROWS)],
            send_sem=send_sem,
            recv_sem=sems.at[slot],
            device_id=to,
            device_id_type=MESH,
        )

    def stay(source, head, target, row, sems, slot):
        return pltpu.make_async_copy(
            source.at[:, column(head)], target.at[pl.ds(pl.multiple_of(row, ROWS), ROWS)], sems.at[slot]
        )

    key_slot, query_slot = 2 + c, (b + 1) % 2

    def scatter_a(tensor, source, target, sems, slot, to_pair):
        row = slot * BLOCK + me * ROWS

        def send(i, _):
            j = (me + 1 + i) % GROUP
            for t in range(2):
                piece(source, 3 * j + t, target, row, sems, slot, (j, owner(t, to_pair)), piece_send.at[tensor]).start()
            return 0

        lax.fori_loop(0, GROUP - 1, send, 0)
        for t in range(2):

            @pl.when(owner(t, to_pair) != b)
            def _():
                piece(source, 3 * me + t, target, row, sems, slot, (me, owner(t, to_pair)), own_send.at[tensor, t]).start()

            @pl.when(owner(t, to_pair) == b)
            def _():
                stay(source, 3 * me + t, target, row, sems, slot).start()

    def scatter_b(tensor, source, target, sems, slot, to_blk, count):
        row = slot * BLOCK + me * ROWS

        def send(i, _):
            j = (me + 1 + i) % GROUP
            piece(source, 3 * j + 2, target, row, sems, slot, (j, to_blk), piece_send.at[tensor]).start()
            return 0

        lax.fori_loop(0, count, send, 0)

    scatter_a(0, k_in, ks, k_sem, key_slot, pair)
    scatter_a(1, v_in, vs, v_sem, key_slot, pair)
    for copy in text_copies:
        copy.wait()
    for u in range(2):
        for i, target in enumerate((tks, tvs)):
            if u:
                exponent = exps[2, i : i + 1, :]
            else:
                exponent = jnp.where(yl == 0, exps[0, i : i + 1, :], exps[1, i : i + 1, :])
            scales = jnp.broadcast_to(jnp.exp2(exponent.astype(F32)), (HD, TEXT)).T
            target[u] = (codes[u, i].astype(F32) * scales).astype(BF16)
    m_s[...] = jnp.full(m_s.shape, -1e30, F32)
    acc_s[...] = jnp.zeros(acc_s.shape, F32)

    def block(ref, slot, rows=BLOCK):
        return ref.at[pl.ds(pl.multiple_of(slot * BLOCK, BLOCK), rows)]

    def arrived(ref, sems, slot):
        pltpu.make_async_copy(block(ref, slot), block(ref, slot), sems.at[slot]).wait()

    def forward(ref, sems, slot, to_slot, to_blk, send):
        return pltpu.make_async_remote_copy(
            src_ref=block(ref, slot),
            dst_ref=block(ref, to_slot),
            send_sem=fwd_send.at[send],
            recv_sem=sems.at[to_slot],
            device_id=(me, to_blk),
            device_id_type=MESH,
        )

    ONE, ZERO, THREE, TWO = A_SLOTS + 1, A_SLOTS, A_SLOTS + 3, A_SLOTS + 2
    forwards_a, forwards_even, forwards_odd, relays = [], [], [], []
    for i, (ref, sems) in enumerate(((ks, k_sem), (vs, v_sem))):
        forwards_a.append((
            forward(ref, sems, 2, 0, next_a, 7 * i),
            forward(ref, sems, 3, 1, next_a, 7 * i + 1),
            forward(ref, sems, 2, 4, prev_a, 7 * i + 2),
        ))
        forwards_even.append((
            forward(ref, sems, TWO, ZERO, after2, 7 * i + 3),
            forward(ref, sems, TWO, THREE, before, 7 * i + 4),
            forward(ref, sems, TWO, ONE, after, 7 * i + 5),
        ))
        forwards_odd.append((
            forward(ref, sems, TWO, ZERO, after2, 7 * i + 3),
            forward(ref, sems, TWO, THREE, before, 7 * i + 4),
        ))
        relays.append(forward(ref, sems, ZERO, ONE, before, 7 * i + 6))

    def pass_on_a(i, ref, sems):
        arrived(ref, sems, 2)
        forwards_a[i][0].start()
        forwards_a[i][2].start()
        arrived(ref, sems, 3)
        forwards_a[i][1].start()

    def pass_on_b(i, ref, sems):
        arrived(ref, sems, TWO)
        forwards_a[i][0].wait_send()
        forwards_a[i][1].wait_send()

        @pl.when(c == 0)
        def _():
            for copy in forwards_even[i]:
                copy.start()

        @pl.when(c == 1)
        def _():
            for copy in forwards_odd[i]:
                copy.start()

    def attend(query, keys, values, chunks):
        for i in range(BLOCK // TILE):
            rows = pl.ds(pl.multiple_of(query * BLOCK + i * TILE, TILE), TILE)
            q, m, acc = qs[rows, :], m_s[rows, :], acc_s[rows, :]
            for at, size in chunks:
                span = pl.ds(pl.multiple_of(at, size), size)
                k, v = keys[span, :], values[span, :]
                s = lax.dot_general(q, k, (((1,), (1,)), ((), ())), preferred_element_type=F32)
                m_new = jnp.maximum(m, jnp.max(s, axis=1, keepdims=True))
                p = jnp.exp2((s - jnp.concatenate([m_new] * (size // HD), axis=1)) * SCALE).astype(BF16)
                alpha = jnp.exp2((m - m_new) * SCALE)
                wide = jnp.concatenate([v, jnp.ones((size, HD), BF16)], axis=1)
                acc = acc * jnp.concatenate([alpha, alpha], axis=1) + jnp.dot(p, wide, preferred_element_type=F32)
                m = m_new
            m_s[rows, :] = m
            acc_s[rows, :] = acc

    def image(query, slot):
        attend(query, ks, vs, [(slot * BLOCK + n * CHUNK, CHUNK) for n in range(BLOCK // CHUNK)])

    def text(query, unit):
        attend(query, tks.at[unit], tvs.at[unit], [(0, TEXT)])

    def result(query, r, head, to_blk, send_sem):
        rows = pl.ds(pl.multiple_of(query * BLOCK + r * ROWS, ROWS), ROWS)
        return pltpu.make_async_remote_copy(
            src_ref=o_s.at[rows],
            dst_ref=out.at[:, column(head)],
            send_sem=send_sem,
            recv_sem=out_sem.at[0],
            device_id=(r, to_blk),
            device_id_type=MESH,
        )

    def finish(query, head, to_blk, count):
        rows = pl.ds(query * BLOCK, BLOCK)
        o_s[rows, :] = (acc_s[rows, :HD] / acc_s[rows, HD:]).astype(BF16)

        def send(i, _):
            result(query, (me + 1 + i) % GROUP, head, to_blk, o_send.at[query]).start()
            return 0

        lax.fori_loop(0, count, send, 0)

    def finish_a(query):
        head, to_blk = 3 * me + yl, (mine * 2 + 1 + query) % N_BLK
        finish(query, head, to_blk, GROUP - 1)

        @pl.when(to_blk != b)
        def _():
            result(query, me, head, to_blk, o_own_send.at[query]).start()

        @pl.when(to_blk == b)
        def _():
            rows = pl.ds(pl.multiple_of(query * BLOCK + me * ROWS, ROWS), ROWS)
            pltpu.make_async_copy(o_s.at[rows], out.at[:, column(head)], out_sem.at[0]).start()

    def own_blocks(query):
        def step(slot, _):
            image(query, slot)
            return 0

        lax.fori_loop(2, 4, step, 0)

    pass_on_a(0, ks, k_sem)
    scatter_a(2, q_in, qs, q_sem, query_slot, pair_q)
    pass_on_a(1, vs, v_sem)
    scatter_b(0, k_in, ks, k_sem, A_SLOTS + 2, b, GROUP - 1)
    stay(k_in, 3 * me + 2, ks, (A_SLOTS + 2) * BLOCK + me * ROWS, k_sem, A_SLOTS + 2).start()
    scatter_b(1, v_in, vs, v_sem, A_SLOTS + 2, b, GROUP - 1)
    stay(v_in, 3 * me + 2, vs, (A_SLOTS + 2) * BLOCK + me * ROWS, v_sem, A_SLOTS + 2).start()
    scatter_b(2, q_in, qs, q_sem, 2, before, GROUP)
    arrived(qs, q_sem, 0)
    own_blocks(0)
    text(0, 0)
    pass_on_b(0, ks, k_sem)
    arrived(qs, q_sem, 1)
    own_blocks(1)
    text(1, 0)
    pass_on_b(1, vs, v_sem)
    arrived(qs, q_sem, 2)
    text(2, 1)

    image(2, TWO)
    arrived(ks, k_sem, 4)
    arrived(vs, v_sem, 4)
    image(1, 4)
    arrived(ks, k_sem, THREE)
    arrived(vs, v_sem, THREE)
    image(2, THREE)

    @pl.when(c == 1)
    def _():
        arrived(ks, k_sem, ONE)
        arrived(vs, v_sem, ONE)
        image(2, ONE)

    arrived(ks, k_sem, 1)
    arrived(vs, v_sem, 1)

    def step_one(query, _):
        image(query, 1)
        return 0

    lax.fori_loop(0, 2, step_one, 0)
    finish_a(1)
    arrived(ks, k_sem, 0)
    arrived(vs, v_sem, 0)
    image(0, 0)
    finish_a(0)

    arrived(ks, k_sem, ZERO)

    @pl.when(c == 1)
    def _():
        relays[0].start()

    arrived(vs, v_sem, ZERO)

    @pl.when(c == 1)
    def _():
        relays[1].start()

    image(2, ZERO)

    @pl.when(c == 0)
    def _():
        arrived(ks, k_sem, ONE)
        arrived(vs, v_sem, ONE)
        image(2, ONE)

    finish(2, 3 * me + 2, after, GROUP)

    def sent(sem, ref):
        pltpu.make_async_copy(ref, ref, sem).wait()

    sent(piece_send.at[0], ks.at[pl.ds(0, 21 * ROWS)])
    sent(piece_send.at[1], ks.at[pl.ds(0, 21 * ROWS)])
    sent(piece_send.at[2], ks.at[pl.ds(0, 22 * ROWS)])
    for tensor, to_pair in ((0, pair), (1, pair), (2, pair_q)):
        for t in range(2):

            @pl.when(owner(t, to_pair) != b)
            def _():
                sent(own_send.at[tensor, t], ks.at[pl.ds(0, ROWS)])

    for i in range(2):
        forwards_a[i][2].wait_send()

        @pl.when(c == 0)
        def _():
            for copy in forwards_even[i]:
                copy.wait_send()

        @pl.when(c == 1)
        def _():
            for copy in forwards_odd[i]:
                copy.wait_send()
            relays[i].wait_send()

    for query in range(2):
        sent(o_send.at[query], o_s.at[pl.ds(0, (GROUP - 1) * ROWS)])

        @pl.when((mine * 2 + 1 + query) % N_BLK != b)
        def _():
            sent(o_own_send.at[query], o_s.at[pl.ds(0, ROWS)])

    sent(o_send.at[2], o_s.at[pl.ds(0, GROUP * ROWS)])
    pltpu.make_async_copy(out, out, out_sem.at[0]).wait()


def local(queries, keys, values, text_codes, text_exps):
    slots = A_SLOTS + B_SLOTS
    dma = pltpu.SemaphoreType.DMA
    return pl.pallas_call(
        kernel,
        out_shape=jax.ShapeDtypeStruct(queries.shape, BF16),
        in_specs=[pl.BlockSpec(memory_space=pl.ANY)] * 5,
        out_specs=pl.BlockSpec(memory_space=pl.ANY),
        scratch_shapes=[
            pltpu.VMEM((3 * BLOCK, HD), BF16),
            pltpu.VMEM((slots * BLOCK, HD), BF16),
            pltpu.VMEM((slots * BLOCK, HD), BF16),
            pltpu.VMEM((2, TEXT, HD), BF16),
            pltpu.VMEM((2, TEXT, HD), BF16),
            pltpu.VMEM((2, 2, TEXT, HD), jnp.int32),
            pltpu.VMEM((3, 2, TEXT), jnp.int32),
            pltpu.VMEM((3 * BLOCK, HD), F32),
            pltpu.VMEM((3 * BLOCK, 2 * HD), F32),
            pltpu.VMEM((3 * BLOCK, HD), BF16),
            dma((3,)),
            dma((slots,)),
            dma((slots,)),
            dma((3,)),
            dma((1,)),
            dma((3,)),
            dma((3, 2)),
            dma((14,)),
            dma((3,)),
            dma((2,)),
        ],
        compiler_params=pltpu.CompilerParams(collective_id=0, has_side_effects=True, vmem_limit_bytes=63 << 20),
        cost_estimate=pl.CostEstimate(flops=7 * 10**9, bytes_accessed=4 * 10**6, transcendentals=14 * 10**6),
    )(queries, keys, values, text_codes, jnp.transpose(text_exps, (2, 0, 1)))


def solution(mesh):
    rows = P(("blk", "head"), None)
    text = P(None, None, "head")
    return jax.shard_map(
        local, mesh=mesh, in_specs=(rows, rows, rows, text, text), out_specs=rows, check_vma=False
    )
```

```python
import math

import jax
import jax.numpy as jnp
from jax import lax
from jax.experimental import pallas as pl
from jax.experimental.pallas import tpu as pltpu
from jax.sharding import PartitionSpec as P

HD = 128
ROWS = 128
BLOCK = 1024
TEXT = 256
GROUP = 8
N_BLK = 32
PAIRS = 16
A_SLOTS, B_SLOTS = 5, 4
TILE = 256
CHUNK = 512
MESH = pl.DeviceIdType.MESH
SCALE = math.log2(math.e) / math.sqrt(HD)
BF16, F32 = jnp.bfloat16, jnp.float32


def owner(t, p):
    return (t * 8 + p % 8) * 2 + p // 8


def kernel(
    q_in, k_in, v_in, codes_in, exps_in, out,
    qs, ks, vs, tks, tvs, codes, exps, m_s, acc_s, o_s,
    text_sem, k_sem, v_sem, q_sem, out_sem,
    piece_send, own_send, fwd_send, o_send, o_own_send,
):
    me = lax.axis_index("head")
    b = lax.axis_index("blk")
    yl, z, c = b // 16, (b // 2) % 8, b % 2
    pair, pair_q = b // 2, ((b + N_BLK - 1) % N_BLK) // 2
    mine = c * 8 + z
    after, after2 = (b + 1) % N_BLK, (b + 2) % N_BLK
    before, before2 = (b + N_BLK - 1) % N_BLK, (b + N_BLK - 2) % N_BLK
    next_a, prev_a = owner(yl, (mine + 1) % PAIRS), owner(yl, (mine + PAIRS - 1) % PAIRS)

    text_copies = [
        pltpu.make_async_copy(codes_in.at[:, :, pl.ds(pl.multiple_of(yl * HD, HD), HD)], codes.at[0], text_sem.at[0]),
        pltpu.make_async_copy(codes_in.at[:, :, pl.ds(2 * HD, HD)], codes.at[1], text_sem.at[1]),
        pltpu.make_async_copy(exps_in, exps, text_sem.at[2]),
    ]
    for copy in text_copies:
        copy.start()

    barrier = pltpu.get_barrier_semaphore()

    def tell(head, blk):
        pl.semaphore_signal(barrier, inc=1, device_id=(head, blk), device_id_type=MESH)

    def greet(i, _):
        other = (me + 1 + i) % GROUP
        for d in range(3):
            tell(other, (mine * 2 + d) % N_BLK)
        tell(other, b)
        tell(other, after)
        tell(other, before)
        for t in range(2):
            tell(other, owner(t, pair_q))
        return 0

    lax.fori_loop(0, GROUP - 1, greet, 0)
    for d in range(3):

        @pl.when((mine * 2 + d) % N_BLK != b)
        def _():
            tell(me, (mine * 2 + d) % N_BLK)

    for t in range(2):

        @pl.when(owner(t, pair_q) != b)
        def _():
            tell(me, owner(t, pair_q))

    tell(me, after)
    tell(me, before)
    tell(me, before2)
    tell(me, next_a)
    tell(me, prev_a)
    expected = 16 * (2 - c) + 7 + 8 + 16 + 8 + 3
    expected = expected - jnp.where(yl == c, 1, 0) - jnp.where((yl == 1) & (c == 1), 1, 0)
    pl.semaphore_wait(barrier, expected)

    def column(head):
        return pl.ds(pl.multiple_of(head * HD, HD), HD)

    def piece(source, head, target, row, sems, slot, to, send_sem):
        return pltpu.make_async_remote_copy(
            src_ref=source.at[:, column(head)],
            dst_ref=target.at[pl.ds(pl.multiple_of(row, ROWS), ROWS)],
            send_sem=send_sem,
            recv_sem=sems.at[slot],
            device_id=to,
            device_id_type=MESH,
        )

    def stay(source, head, target, row, sems, slot):
        return pltpu.make_async_copy(
            source.at[:, column(head)], target.at[pl.ds(pl.multiple_of(row, ROWS), ROWS)], sems.at[slot]
        )

    key_slot, query_slot = 2 + c, (b + 1) % 2

    def scatter_a(tensor, source, target, sems, slot, to_pair):
        row = slot * BLOCK + me * ROWS

        def send(i, _):
            j = (me + 1 + i) % GROUP
            for t in range(2):
                piece(source, 3 * j + t, target, row, sems, slot, (j, owner(t, to_pair)), piece_send.at[tensor]).start()
            return 0

        lax.fori_loop(0, GROUP - 1, send, 0)
        for t in range(2):

            @pl.when(owner(t, to_pair) != b)
            def _():
                piece(source, 3 * me + t, target, row, sems, slot, (me, owner(t, to_pair)), own_send.at[tensor, t]).start()

            @pl.when(owner(t, to_pair) == b)
            def _():
                stay(source, 3 * me + t, target, row, sems, slot).start()

    def scatter_b(tensor, source, target, sems, slot, to_blk, count):
        row = slot * BLOCK + me * ROWS

        def send(i, _):
            j = (me + 1 + i) % GROUP
            piece(source, 3 * j + 2, target, row, sems, slot, (j, to_blk), piece_send.at[tensor]).start()
            return 0

        lax.fori_loop(0, count, send, 0)

    scatter_a(0, k_in, ks, k_sem, key_slot, pair)
    scatter_a(1, v_in, vs, v_sem, key_slot, pair)
    for copy in text_copies:
        copy.wait()
    for u in range(2):
        for i, target in enumerate((tks, tvs)):
            if u:
                exponent = exps[2, i : i + 1, :]
            else:
                exponent = jnp.where(yl == 0, exps[0, i : i + 1, :], exps[1, i : i + 1, :])
            scales = jnp.broadcast_to(jnp.exp2(exponent.astype(F32)), (HD, TEXT)).T
            target[u] = (codes[u, i].astype(F32) * scales).astype(BF16)
    m_s[...] = jnp.full(m_s.shape, -1e30, F32)
    acc_s[...] = jnp.zeros(acc_s.shape, F32)

    def block(ref, slot, rows=BLOCK):
        return ref.at[pl.ds(pl.multiple_of(slot * BLOCK, BLOCK), rows)]

    def arrived(ref, sems, slot):
        pltpu.make_async_copy(block(ref, slot), block(ref, slot), sems.at[slot]).wait()

    def forward(ref, sems, slot, to_slot, to_blk, send):
        return pltpu.make_async_remote_copy(
            src_ref=block(ref, slot),
            dst_ref=block(ref, to_slot),
            send_sem=fwd_send.at[send],
            recv_sem=sems.at[to_slot],
            device_id=(me, to_blk),
            device_id_type=MESH,
        )

    ONE, ZERO, THREE, TWO = A_SLOTS + 1, A_SLOTS, A_SLOTS + 3, A_SLOTS + 2
    forwards_a, forwards_even, forwards_odd, relays = [], [], [], []
    for i, (ref, sems) in enumerate(((ks, k_sem), (vs, v_sem))):
        forwards_a.append((
            forward(ref, sems, 2, 0, next_a, 7 * i),
            forward(ref, sems, 3, 1, next_a, 7 * i + 1),
            forward(ref, sems, 2, 4, prev_a, 7 * i + 2),
        ))
        forwards_even.append((
            forward(ref, sems, TWO, ZERO, after2, 7 * i + 3),
            forward(ref, sems, TWO, THREE, before, 7 * i + 4),
            forward(ref, sems, TWO, ONE, after, 7 * i + 5),
        ))
        forwards_odd.append((
            forward(ref, sems, TWO, ZERO, after2, 7 * i + 3),
            forward(ref, sems, TWO, THREE, before, 7 * i + 4),
        ))
        relays.append(forward(ref, sems, ZERO, ONE, before, 7 * i + 6))

    def pass_on_a(i, ref, sems):
        arrived(ref, sems, 2)
        forwards_a[i][0].start()
        forwards_a[i][2].start()
        arrived(ref, sems, 3)
        forwards_a[i][1].start()

    def pass_on_b(i, ref, sems):
        arrived(ref, sems, TWO)

        @pl.when(c == 0)
        def _():
            for copy in forwards_even[i][1:]:
                copy.start()

        @pl.when(c == 1)
        def _():
            for copy in forwards_odd[i][1:]:
                copy.start()

        if i:
            for n in range(2):
                forwards_a[n][0].wait_send()
                forwards_a[n][1].wait_send()
                forwards_even[n][0].start()

    def attend(query, keys, values, chunks):
        for i in range(BLOCK // TILE):
            rows = pl.ds(pl.multiple_of(query * BLOCK + i * TILE, TILE), TILE)
            q, m, acc = qs[rows, :], m_s[rows, :], acc_s[rows, :]
            for at, size in chunks:
                span = pl.ds(pl.multiple_of(at, size), size)
                k, v = keys[span, :], values[span, :]
                s = lax.dot_general(q, k, (((1,), (1,)), ((), ())), preferred_element_type=F32)
                m_new = jnp.maximum(m, jnp.max(s, axis=1, keepdims=True))
                p = jnp.exp2((s - jnp.concatenate([m_new] * (size // HD), axis=1)) * SCALE).astype(BF16)
                alpha = jnp.exp2((m - m_new) * SCALE)
                wide = jnp.concatenate([v, jnp.ones((size, HD), BF16)], axis=1)
                acc = acc * jnp.concatenate([alpha, alpha], axis=1) + jnp.dot(p, wide, preferred_element_type=F32)
                m = m_new
            m_s[rows, :] = m
            acc_s[rows, :] = acc

    def image(query, slot):
        attend(query, ks, vs, [(slot * BLOCK + n * CHUNK, CHUNK) for n in range(BLOCK // CHUNK)])

    def text(query, unit):
        attend(query, tks.at[unit], tvs.at[unit], [(0, TEXT)])

    def result(query, r, head, to_blk, send_sem):
        rows = pl.ds(pl.multiple_of(query * BLOCK + r * ROWS, ROWS), ROWS)
        return pltpu.make_async_remote_copy(
            src_ref=o_s.at[rows],
            dst_ref=out.at[:, column(head)],
            send_sem=send_sem,
            recv_sem=out_sem.at[0],
            device_id=(r, to_blk),
            device_id_type=MESH,
        )

    def finish(query, head, to_blk, count):
        rows = pl.ds(query * BLOCK, BLOCK)
        o_s[rows, :] = (acc_s[rows, :HD] / acc_s[rows, HD:]).astype(BF16)

        def send(i, _):
            result(query, (me + 1 + i) % GROUP, head, to_blk, o_send.at[query]).start()
            return 0

        lax.fori_loop(0, count, send, 0)

    def finish_a(query):
        head, to_blk = 3 * me + yl, (mine * 2 + 1 + query) % N_BLK
        finish(query, head, to_blk, GROUP - 1)

        @pl.when(to_blk != b)
        def _():
            result(query, me, head, to_blk, o_own_send.at[query]).start()

        @pl.when(to_blk == b)
        def _():
            rows = pl.ds(pl.multiple_of(query * BLOCK + me * ROWS, ROWS), ROWS)
            pltpu.make_async_copy(o_s.at[rows], out.at[:, column(head)], out_sem.at[0]).start()

    def own_blocks(query):
        def step(slot, _):
            image(query, slot)
            return 0

        lax.fori_loop(2, 4, step, 0)

    pass_on_a(0, ks, k_sem)
    scatter_a(2, q_in, qs, q_sem, query_slot, pair_q)
    pass_on_a(1, vs, v_sem)
    scatter_b(0, k_in, ks, k_sem, A_SLOTS + 2, b, GROUP - 1)
    stay(k_in, 3 * me + 2, ks, (A_SLOTS + 2) * BLOCK + me * ROWS, k_sem, A_SLOTS + 2).start()
    scatter_b(1, v_in, vs, v_sem, A_SLOTS + 2, b, GROUP - 1)
    stay(v_in, 3 * me + 2, vs, (A_SLOTS + 2) * BLOCK + me * ROWS, v_sem, A_SLOTS + 2).start()
    scatter_b(2, q_in, qs, q_sem, 2, before, GROUP)
    arrived(qs, q_sem, 0)
    own_blocks(0)
    text(0, 0)
    pass_on_b(0, ks, k_sem)
    arrived(qs, q_sem, 1)
    own_blocks(1)
    text(1, 0)
    pass_on_b(1, vs, v_sem)
    arrived(qs, q_sem, 2)
    text(2, 1)

    image(2, TWO)
    arrived(ks, k_sem, 4)
    arrived(vs, v_sem, 4)
    image(1, 4)
    arrived(ks, k_sem, THREE)
    arrived(vs, v_sem, THREE)
    image(2, THREE)

    @pl.when(c == 1)
    def _():
        arrived(ks, k_sem, ONE)
        arrived(vs, v_sem, ONE)
        image(2, ONE)

    arrived(ks, k_sem, 1)
    arrived(vs, v_sem, 1)

    def step_one(query, _):
        image(query, 1)
        return 0

    lax.fori_loop(0, 2, step_one, 0)
    finish_a(1)
    arrived(ks, k_sem, 0)
    arrived(vs, v_sem, 0)
    image(0, 0)
    finish_a(0)

    arrived(ks, k_sem, ZERO)

    @pl.when(c == 1)
    def _():
        relays[0].start()

    arrived(vs, v_sem, ZERO)

    @pl.when(c == 1)
    def _():
        relays[1].start()

    image(2, ZERO)

    @pl.when(c == 0)
    def _():
        arrived(ks, k_sem, ONE)
        arrived(vs, v_sem, ONE)
        image(2, ONE)

    finish(2, 3 * me + 2, after, GROUP)

    def sent(sem, ref):
        pltpu.make_async_copy(ref, ref, sem).wait()

    sent(piece_send.at[0], ks.at[pl.ds(0, 21 * ROWS)])
    sent(piece_send.at[1], ks.at[pl.ds(0, 21 * ROWS)])
    sent(piece_send.at[2], ks.at[pl.ds(0, 22 * ROWS)])
    for tensor, to_pair in ((0, pair), (1, pair), (2, pair_q)):
        for t in range(2):

            @pl.when(owner(t, to_pair) != b)
            def _():
                sent(own_send.at[tensor, t], ks.at[pl.ds(0, ROWS)])

    for i in range(2):
        forwards_a[i][2].wait_send()
        forwards_even[i][0].wait_send()

        @pl.when(c == 0)
        def _():
            for copy in forwards_even[i][1:]:
                copy.wait_send()

        @pl.when(c == 1)
        def _():
            for copy in forwards_odd[i][1:]:
                copy.wait_send()
            relays[i].wait_send()

    for query in range(2):
        sent(o_send.at[query], o_s.at[pl.ds(0, (GROUP - 1) * ROWS)])

        @pl.when((mine * 2 + 1 + query) % N_BLK != b)
        def _():
            sent(o_own_send.at[query], o_s.at[pl.ds(0, ROWS)])

    sent(o_send.at[2], o_s.at[pl.ds(0, GROUP * ROWS)])
    pltpu.make_async_copy(out, out, out_sem.at[0]).wait()


def local(queries, keys, values, text_codes, text_exps):
    slots = A_SLOTS + B_SLOTS
    dma = pltpu.SemaphoreType.DMA
    return pl.pallas_call(
        kernel,
        out_shape=jax.ShapeDtypeStruct(queries.shape, BF16),
        in_specs=[pl.BlockSpec(memory_space=pl.ANY)] * 5,
        out_specs=pl.BlockSpec(memory_space=pl.ANY),
        scratch_shapes=[
            pltpu.VMEM((3 * BLOCK, HD), BF16),
            pltpu.VMEM((slots * BLOCK, HD), BF16),
            pltpu.VMEM((slots * BLOCK, HD), BF16),
            pltpu.VMEM((2, TEXT, HD), BF16),
            pltpu.VMEM((2, TEXT, HD), BF16),
            pltpu.VMEM((2, 2, TEXT, HD), jnp.int32),
            pltpu.VMEM((3, 2, TEXT), jnp.int32),
            pltpu.VMEM((3 * BLOCK, HD), F32),
            pltpu.VMEM((3 * BLOCK, 2 * HD), F32),
            pltpu.VMEM((3 * BLOCK, HD), BF16),
            dma((3,)),
            dma((slots,)),
            dma((slots,)),
            dma((3,)),
            dma((1,)),
            dma((3,)),
            dma((3, 2)),
            dma((14,)),
            dma((3,)),
            dma((2,)),
        ],
        compiler_params=pltpu.CompilerParams(collective_id=0, has_side_effects=True, vmem_limit_bytes=63 << 20),
        cost_estimate=pl.CostEstimate(flops=7 * 10**9, bytes_accessed=4 * 10**6, transcendentals=14 * 10**6),
    )(queries, keys, values, text_codes, jnp.transpose(text_exps, (2, 0, 1)))


def solution(mesh):
    rows = P(("blk", "head"), None)
    text = P(None, None, "head")
    return jax.shard_map(
        local, mesh=mesh, in_specs=(rows, rows, rows, text, text), out_specs=rows, check_vma=False
    )
```
